32 devices in a mesh: grp: 2 (over core), row: 4 (over y, x), col: 4 (over z).
Axes of the slice: x: 2, y: 2, z: 4, core: 2. Of those that a mesh axis runs over, the one named last changes fastest.
Arguments:
- root_inverse: bfloat16 [12288, 12288], P(('grp', 'row'), 'col'), may hold values from -0.0546875 to 0.0546875
- child_inverse: bfloat16 [2, 8192, 8192], P('grp', 'row', 'col'), may hold values from -0.0625 to 0.0625
- coupling: bfloat16 [2, 1536, 8192], P('grp', 'col', 'row'), may hold values from -0.0625 to 0.0625
- child_weights: bfloat16 [2, 8192], P('grp', 'col'), may hold values from 0.5 to 2
- root_weights: bfloat16 [12288], P('col'), may hold values from 0.5 to 2
- parent_blocks: int32 [2, 12], replicated, may hold values from 0 to 95, as said below
Outputs:
- grad_root: bfloat16 [12288, 12288], P(('grp', 'row'), 'col')
- grad_child: bfloat16 [2, 8192, 8192], P('grp', 'row', 'col')
- grad_coupling: bfloat16 [2, 1536, 8192], P('grp', 'col', 'row')
The draws below stay inside these ranges and needn't reach their ends.
Inputs may be any that keep to these rules, and one draw needn't show every extreme that they name: `parent_blocks`: within one child the 12 blocks are distinct; child 0 always names block 0 and block 12288 // 128 - 1; the two children may share blocks.
All inputs are finite; a program needn't handle non-finite values.
Results may differ from the reference program's by a relative error of at most 0.0059.
Values may be sent and summed in bfloat16 or wider, within the bound.
No kernel may reach another device: no remote copies, remote signals or barrier semaphores. Data moves between devices by JAX's collectives and lax.ppermute only.
A program may use at most 128 MiB of HBM per device.

```python
import jax
import jax.numpy as jnp

NR = 12288
NC = 8192
BW = 128
MB = 12
M = 1536


def draw_parent_blocks(key, part):
    total = NR // BW
    inner = jax.random.permutation(jax.random.fold_in(key, 11), total - 2)[:MB - 2] + 1
    first = jnp.concatenate([jnp.zeros((1,), jnp.int32), inner.astype(jnp.int32), jnp.full((1,), total - 1, jnp.int32)])
    second = jax.random.permutation(jax.random.fold_in(key, 12), total)[:MB].astype(jnp.int32)
    return jnp.stack([first, second]).astype(jnp.int32)


def shard_levels(own_key, shape, shards, least, largest):
    def one(axis_at, shards_of):
        steps = jax.random.uniform(jax.random.fold_in(jax.random.fold_in(own_key, 6), axis_at), (shards_of,), jnp.float32, least / len(shards), largest / len(shards))
        return jnp.repeat(jnp.exp(steps), shape[axis_at] // shards_of).reshape((-1,) + (1,) * (len(shape) - axis_at - 1))

    loudness = one(*shards[0])
    for cut in shards[1:]:
        loudness = loudness * one(*cut)
    return loudness


def noise(key, shape, deviation, limit, pieces=(), held_as=jnp.bfloat16):
    array = deviation * jax.random.normal(key, shape, jnp.float32)
    if pieces:
        array = array * shard_levels(key, shape, pieces, -0.22, 0.18)
    return jnp.clip(array, -limit, limit).astype(held_as)


def setup_inputs(seed: int = 0) -> dict:
    seeds = jax.random.split(jax.random.key(seed), 7)
    return {
        "root_inverse": noise(seeds[0], (NR, NR), NR ** -0.5, 0.0546875, ((0, 8), (1, 4))),
        "child_inverse": noise(seeds[1], (2, NC, NC), NC ** -0.5, 0.0625, ((0, 2), (1, 4), (2, 4))),
        "coupling": noise(seeds[2], (2, M, NC), NC ** -0.5, 0.0625, ((0, 2), (1, 4), (2, 4))),
        "child_weights": jnp.clip(0.5 + 1.5 * jax.random.uniform(seeds[3], (2, NC), jnp.float32) ** shard_levels(seeds[3], (2, NC), ((0, 2), (1, 4)), -0.2, 0.2), 0.5, 2.0).astype(jnp.bfloat16),
        "root_weights": jnp.clip(0.5 + 1.5 * jax.random.uniform(seeds[4], (NR,), jnp.float32) ** shard_levels(seeds[4], (NR,), ((0, 4),), -0.2, 0.2), 0.5, 2.0).astype(jnp.bfloat16),
        "parent_blocks": draw_parent_blocks(jax.random.fold_in(seeds[6], 71), 0),
    }


def matmul(left, right):
    return jnp.dot(left.astype(jnp.float32), right.astype(jnp.float32), preferred_element_type=jnp.float32)


def reference(root_inverse, child_inverse, coupling, child_weights, root_weights, parent_blocks):
    offsets = jnp.arange(BW, dtype=jnp.int32)
    grad_root = 2.0 * root_inverse.astype(jnp.float32) * root_weights.astype(jnp.float32)[None, :]
    grads_factor = []
    grads_links = []
    for child in range(2):
        columns = (parent_blocks[child][:, None].astype(jnp.int32) * BW + offsets[None, :]).reshape(-1).astype(jnp.int32)
        selected = jnp.take(root_inverse, columns, axis=1)
        margin = matmul(selected.T, selected).astype(jnp.bfloat16)
        factor = child_inverse[child]
        links = coupling[child]
        weights = child_weights[child].astype(jnp.float32)
        solved = matmul(links, factor).astype(jnp.bfloat16)
        scaled = (solved.astype(jnp.float32) * weights[None, :]).astype(jnp.bfloat16)
        adjoint = matmul(scaled, solved.T).astype(jnp.bfloat16)
        lifted = matmul(selected, adjoint).astype(jnp.bfloat16)
        grad_root = grad_root.at[:, columns].add(2.0 * lifted.astype(jnp.float32))
        pulled = (2.0 * matmul(margin, solved) * weights[None, :]).astype(jnp.bfloat16)
        grads_links.append(matmul(pulled, factor.T).astype(jnp.bfloat16))
        grad_factor = matmul(links.T, pulled) + 2.0 * factor.astype(jnp.float32) * weights[None, :]
        grads_factor.append(grad_factor.astype(jnp.bfloat16))
    return grad_root.astype(jnp.bfloat16), jnp.stack(grads_factor), jnp.stack(grads_links)
```

```python
import functools

import jax
import jax.numpy as jnp
from jax import lax
from jax.experimental import pallas as pl
from jax.experimental.pallas import tpu as pltpu
from jax.sharding import PartitionSpec as P

BW = 128
F32 = jnp.float32
BF16 = jnp.bfloat16


def mm(a, b, contract):
    return lax.dot_general(a, b, (contract, ((), ())), preferred_element_type=F32)


def pick_kernel(place, owned, root_ref, out_ref):
    s = pl.program_id(0)

    @pl.when(owned[s] == 1)
    def _():
        out_ref[...] = root_ref[...]

    @pl.when(owned[s] == 0)
    def _():
        out_ref[...] = jnp.zeros_like(out_ref)


def pick(root, place, owned):
    rows, slots = root.shape[0], place.shape[0]
    return pl.pallas_call(
        pick_kernel,
        grid_spec=pltpu.PrefetchScalarGridSpec(
            num_scalar_prefetch=2,
            grid=(slots,),
            in_specs=[pl.BlockSpec((rows, BW), lambda s, place, owned: (0, place[s]))],
            out_specs=pl.BlockSpec((rows, BW), lambda s, place, owned: (0, s)),
        ),
        out_shape=jax.ShapeDtypeStruct((rows, slots * BW), BF16),
        cost_estimate=pl.CostEstimate(
            flops=0, bytes_accessed=2 * rows * slots * BW * 2, transcendentals=0
        ),
    )(place, owned, root)


def finish_kernel(
    share,
    at,
    has,
    spot,
    root_ref,
    weight_ref,
    mine_ref,
    other_ref,
    s0,
    s1,
    s2,
    s3,
    out_ref,
):
    block = pl.program_id(0)
    width = mine_ref.shape[0]
    out_ref[...] = (2.0 * root_ref[...].astype(F32) * weight_ref[...].astype(F32)).astype(BF16)

    @pl.when(has[0, block] + has[1, block] > 0)
    def _():
        scale = weight_ref[...].astype(F32)
        for index, part in enumerate((s0, s1, s2, s3)):
            start = pl.multiple_of(spot[index] * share, share)
            rows = pl.ds(start, share)
            out = 2.0 * root_ref[rows, :].astype(F32) * scale
            for which, adjoint in enumerate((mine_ref, other_ref)):
                column = pl.multiple_of(spot[4 + which] * width, BW)
                lifted = jnp.dot(
                    part[:, pl.ds(column, width)], adjoint[...], preferred_element_type=F32
                ).astype(BF16)
                keep = jnp.where(has[which, block] == 1, 2.0, 0.0).astype(F32)
                out = out + keep * lifted.astype(F32)
            out_ref[rows, :] = out.astype(BF16)


def finish(root, weights, mine, other, parts, at, has, spot):
    rows, columns = root.shape
    blocks = columns // BW
    width = mine.shape[0]
    share = parts[0].shape[0]
    whole = pl.BlockSpec(parts[0].shape, lambda b, at, has, spot: (0, 0))
    return pl.pallas_call(
        functools.partial(finish_kernel, share),
        grid_spec=pltpu.PrefetchScalarGridSpec(
            num_scalar_prefetch=3,
            grid=(blocks,),
            in_specs=[
                pl.BlockSpec((rows, BW), lambda b, at, has, spot: (0, b)),
                pl.BlockSpec((1, BW), lambda b, at, has, spot: (0, b)),
                pl.BlockSpec((width, BW), lambda b, at, has, spot: (0, at[0, b])),
                pl.BlockSpec((width, BW), lambda b, at, has, spot: (0, at[1, b])),
                whole,
                whole,
                whole,
                whole,
            ],
            out_specs=pl.BlockSpec((rows, BW), lambda b, at, has, spot: (0, b)),
        ),
        out_shape=jax.ShapeDtypeStruct((rows, columns), BF16),
        compiler_params=pltpu.CompilerParams(vmem_limit_bytes=48 * 2**20),
        cost_estimate=pl.CostEstimate(
            flops=2 * rows * width * width,
            bytes_accessed=2 * rows * (2 * columns + 2 * width) * 2,
            transcendentals=0,
        ),
    )(at, has, spot, root, weights, mine, other, *parts)


def swap(x, axis, d):
    n = lax.axis_size(axis)
    return lax.ppermute(x, axis, [(i, i ^ d) for i in range(n)])


FAR, MIDDLE, NEAR = (3, 3, 0, 0), (2, 2, 1, 1), (1, 0, 3, 2)


def up(x, lo, hi):
    return lax.ppermute(x, "col", [(i, i + 1) for i in range(lo, hi + 1)])


def down(x, lo, hi):
    return lax.ppermute(x, "col", [(i, i - 1) for i in range(lo, hi + 1)])


def line_gather(x, z):
    up1, down1 = up(x, 0, 2), down(x, 1, 3)
    near = jnp.where(z % 2 == 0, down1, up1)
    up2, down2 = up(up1, 1, 2), down(down1, 1, 2)
    middle = jnp.where(z < 2, jnp.where(z == 0, down2, down1), jnp.where(z == 2, up1, up2))
    up3, down3 = up(up2, 2, 2), down(down2, 1, 1)
    far = jnp.where(z < 2, jnp.where(z == 0, down3, down2), jnp.where(z == 2, up2, up3))
    return [far, middle, near, x]


def line_scatter(chunks, z, join):
    far, middle, near, own = chunks
    up1, down1 = up(far, 0, 0), down(far, 3, 3)
    up2 = up(join(jnp.where(z == 0, middle, far), up1), 0, 1)
    down2 = down(join(jnp.where(z == 3, middle, far), down1), 2, 3)
    up3 = up(join(jnp.where(z == 1, middle, near), up2), 0, 2)
    down3 = down(join(jnp.where(z == 2, middle, near), down2), 1, 3)
    return join(join(own, up3), down3)


def add(a, b):
    return (a.astype(F32) + b.astype(F32)).astype(BF16)


def row_scatter(chunk, r, n):
    if n != 4:
        parts = jnp.stack([chunk(i).astype(BF16) for i in range(n)])
        return lax.psum_scatter(parts, "row", scatter_dimension=0, tiled=False).astype(F32)
    arrived = [swap(chunk(r ^ d).astype(BF16), "row", d) for d in (1, 2, 3)]
    return sum((a.astype(F32) for a in arrived), chunk(r).astype(F32))


def row_gather(x, r, n, axis):
    if n != 4:
        return lax.all_gather(x, "row", axis=axis, tiled=True)
    shape = list(x.shape)
    step = shape[axis]
    shape[axis] = step * n
    whole = jnp.zeros(shape, x.dtype)
    for d in range(n):
        piece = swap(x, "row", d) if d else x
        whole = lax.dynamic_update_slice_in_dim(whole, piece, (r ^ d) * step, axis)
    return whole


def col_sum(x, z):
    n = lax.axis_size("col")
    step = x.shape[0] // n
    piece = lambda i: lax.dynamic_slice_in_dim(x, i * step, step, 0)
    arrived = [swap(piece(z ^ d).astype(BF16), "col", d) for d in range(1, n)]
    total = sum((a.astype(F32) for a in arrived), piece(z)).astype(BF16)
    whole = jnp.zeros(x.shape, BF16)
    for d in range(n):
        part = swap(total, "col", d) if d else total
        whole = lax.dynamic_update_slice_in_dim(whole, part, (z ^ d) * step, 0)
    return whole


def local(root, child_inverse, coupling, child_weights, root_weights, parent_blocks):
    g, r, z = lax.axis_index("grp"), lax.axis_index("row"), lax.axis_index("col")
    nrow, ncol = lax.axis_size("row"), lax.axis_size("col")
    root_rows, root_cols = root.shape
    blocks = root_cols // BW
    factor, links = child_inverse[0], coupling[0]
    weights = child_weights[0].astype(F32)
    share = links.shape[0]
    width = share * ncol
    count = width // BW
    cols = factor.shape[1]
    sub = cols // nrow
    strip = width // nrow
    order = [jnp.array(t, jnp.int32)[z] for t in (FAR, MIDDLE, NEAR)] + [z]

    offset = parent_blocks.reshape(-1) - z * blocks
    owned = (offset >= 0) & (offset < blocks)
    picked = pick(root, jnp.clip(offset, 0, blocks - 1), owned.astype(jnp.int32))
    band = root_rows // ncol
    rows_of = lambda q: lax.dynamic_slice_in_dim(picked, q * band, band, 0)
    selected = line_scatter([rows_of(q) for q in order], z, jnp.add)

    mine = lax.dynamic_slice_in_dim(selected, g * width, width, 1)
    other = lax.dynamic_slice_in_dim(selected, (1 - g) * width, width, 1)
    theirs = swap(mm(other, other, ((0,), (0,))).astype(BF16), "grp", 1)

    def margin_rows(i):
        left = lax.dynamic_slice_in_dim(mine, i * strip, strip, 1)
        there = lax.dynamic_slice_in_dim(theirs, i * strip, strip, 0)
        return mm(left, mine, ((0,), (0,))) + there.astype(F32)

    margin = row_gather(col_sum(row_scatter(margin_rows, r, nrow), z), r, nrow, 0)

    links_parts = line_gather(links, z)
    solved = jnp.zeros((width, sub), BF16)
    for q, part in zip(reversed(order), reversed(links_parts)):
        product = mm(part, factor, ((1,), (0,)))
        piece = row_scatter(
            lambda i: lax.dynamic_slice_in_dim(product, i * sub, sub, 1), r, nrow
        ).astype(BF16)
        solved = lax.dynamic_update_slice_in_dim(solved, piece, q * share, 0)
    my_weights = lax.dynamic_slice_in_dim(weights, r * sub, sub, 0)[None, :]
    scaled = (solved.astype(F32) * my_weights).astype(BF16)

    pulled_parts, partial = [], []
    for q in order:
        left = lax.dynamic_slice_in_dim(margin, q * share, share, 0)
        pulled = (2.0 * mm(left, solved, ((1,), (0,))) * my_weights).astype(BF16)
        pulled = row_gather(pulled, r, nrow, 1)
        pulled_parts.append(pulled)
        partial.append(mm(pulled, factor, ((1,), (1,))).astype(BF16))
    grad_links = line_scatter(partial, z, add)

    def adjoint_rows(i):
        return mm(lax.dynamic_slice_in_dim(scaled, i * strip, strip, 0), solved, ((1,), (1,)))

    adjoint = row_gather(col_sum(row_scatter(adjoint_rows, r, nrow), z), r, nrow, 0)
    adjoint_other = swap(adjoint, "grp", 1)

    grad_factor = mm(
        jnp.concatenate(links_parts, axis=0),
        jnp.concatenate(pulled_parts, axis=0),
        ((0,), (0,)),
    )
    grad_factor = (grad_factor + 2.0 * factor.astype(F32) * weights[None, :]).astype(BF16)

    parts = line_gather(selected, z)
    offset = offset.reshape(2, count)
    children = jnp.stack([g, 1 - g])
    match = offset[children][:, :, None] == jnp.arange(blocks, dtype=jnp.int32)[None, None, :]
    has = jnp.any(match, axis=1).astype(jnp.int32)
    at = jnp.argmax(match, axis=1).astype(jnp.int32)
    spot = jnp.stack(order + [g, 1 - g]).astype(jnp.int32)
    grad_root = finish(root, root_weights[None, :], adjoint, adjoint_other, parts, at, has, spot)
    return (grad_root, grad_factor[None], grad_links[None])


def solution(mesh):
    return jax.shard_map(
        local,
        mesh=mesh,
        in_specs=(
            P(("grp", "row"), "col"),
            P("grp", "row", "col"),
            P("grp", "col", "row"),
            P("grp", "col"),
            P("col"),
            P(),
        ),
        out_specs=(P(("grp", "row"), "col"), P("grp", "row", "col"), P("grp", "col", "row")),
        check_vma=False,
    )
```

```python
import functools

import jax
import jax.numpy as jnp
from jax import lax
from jax.experimental import pallas as pl
from jax.experimental.pallas import tpu as pltpu
from jax.sharding import PartitionSpec as P

BW = 128
F32 = jnp.float32
BF16 = jnp.bfloat16
I32 = jnp.int32
VMEM = 48 * 2**20


def mm(a, b, contract):
    return lax.dot_general(a, b, (contract, ((), ())), preferred_element_type=F32)


def take(x, start, size, axis):
    return lax.dynamic_slice_in_dim(x, start, size, axis)


def after(x, *others):
    return lax.optimization_barrier((x, *others))[0]


def swap(x, axis, d):
    n = lax.axis_size(axis)
    return lax.ppermute(x, axis, [(i, i ^ d) for i in range(n)])


def pick_kernel(band, place, spot, root_ref, *outs):
    for d, out in enumerate(outs):
        out[...] = root_ref[pl.ds(pl.multiple_of(spot[d] * band, band), band), :]


def pick(root, place, spot, parts):
    rows, count = root.shape[0], place.shape[0]
    band = rows // parts
    return pl.pallas_call(
        functools.partial(pick_kernel, band),
        grid_spec=pltpu.PrefetchScalarGridSpec(
            num_scalar_prefetch=2,
            grid=(count,),
            in_specs=[pl.BlockSpec((rows, BW), lambda k, place, spot: (0, place[k]))],
            out_specs=[pl.BlockSpec((band, BW), lambda k, place, spot: (0, k))] * parts,
        ),
        out_shape=[jax.ShapeDtypeStruct((band, count * BW), BF16)] * parts,
        cost_estimate=pl.CostEstimate(
            flops=0, bytes_accessed=4 * rows * count * BW, transcendentals=0
        ),
    )(place, spot, root)


def assemble_kernel(source, rank, *refs):
    pieces, out = refs[:-1], refs[-1]
    slots = out.shape[1] // BW
    for s in range(slots):
        for d, piece in enumerate(pieces):

            @pl.when(source[s] == d)
            def _():
                start = pl.multiple_of(rank[s] * BW, BW)
                out[:, s * BW : (s + 1) * BW] = piece[:, pl.ds(start, BW)]


def assemble(pieces, source, rank):
    band, slots = pieces[0].shape[0], source.shape[0]
    whole = lambda shape: pl.BlockSpec(shape, lambda i, source, rank: (0, 0))
    return pl.pallas_call(
        assemble_kernel,
        grid_spec=pltpu.PrefetchScalarGridSpec(
            num_scalar_prefetch=2,
            grid=(1,),
            in_specs=[whole(p.shape) for p in pieces],
            out_specs=whole((band, slots * BW)),
        ),
        out_shape=jax.ShapeDtypeStruct((band, slots * BW), BF16),
        compiler_params=pltpu.CompilerParams(vmem_limit_bytes=VMEM),
        cost_estimate=pl.CostEstimate(
            flops=0, bytes_accessed=6 * band * slots * BW, transcendentals=0
        ),
    )(source, rank, *pieces)


def unfold_kernel(count, half, packed_ref, out_ref):
    i = pl.program_id(0)
    for d in range(half + 1):
        j = lax.rem(i + d, count)
        out_ref[:, pl.ds(pl.multiple_of(j * BW, BW), BW)] = packed_ref[
            pl.ds(pl.multiple_of(i * BW, BW), BW), d * BW : (d + 1) * BW
        ]
    for d in range(1, count - half):
        j = lax.rem(i + count - d, count)
        block = packed_ref[pl.ds(pl.multiple_of(j * BW, BW), BW), d * BW : (d + 1) * BW]
        out_ref[:, pl.ds(pl.multiple_of(j * BW, BW), BW)] = block.T


def unfold(packed):
    width = packed.shape[0]
    count = width // BW
    return pl.pallas_call(
        functools.partial(unfold_kernel, count, count // 2),
        grid=(count,),
        in_specs=[pl.BlockSpec(packed.shape, lambda i: (0, 0))],
        out_specs=pl.BlockSpec((BW, width), lambda i: (i, 0)),
        out_shape=jax.ShapeDtypeStruct((width, width), BF16),
        compiler_params=pltpu.CompilerParams(vmem_limit_bytes=VMEM),
        cost_estimate=pl.CostEstimate(
            flops=0, bytes_accessed=4 * width * width, transcendentals=0
        ),
    )(packed)


def finish_kernel(block, at, has, root_ref, weight_ref, mine_ref, other_ref, all_ref, base, out_ref):
    k = pl.program_id(0)
    width = mine_ref.shape[0]

    @pl.when((k == 0) | (block[k] != block[lax.max(k - 1, 0)]))
    def _():
        out = 2.0 * root_ref[...].astype(F32) * weight_ref[...].astype(F32)
        for w, adjoint in enumerate((mine_ref, other_ref)):
            lifted = jnp.dot(
                all_ref[:, w * width : (w + 1) * width],
                adjoint[...],
                preferred_element_type=F32,
            )
            keep = jnp.where(has[w, k] == 1, 2.0, 0.0).astype(F32)
            out = out + keep * lifted.astype(BF16).astype(F32)
        out_ref[...] = out.astype(BF16)


def finish(base, root, weights, mine, other, selected, block, at, has):
    rows = root.shape[0]
    width = mine.shape[0]
    steps = block.shape[0]
    strip = pl.BlockSpec((rows, BW), lambda k, block, at, has: (0, block[k]))
    return pl.pallas_call(
        finish_kernel,
        grid_spec=pltpu.PrefetchScalarGridSpec(
            num_scalar_prefetch=3,
            grid=(steps,),
            in_specs=[
                strip,
                pl.BlockSpec((1, BW), lambda k, block, at, has: (0, block[k])),
                pl.BlockSpec((width, BW), lambda k, block, at, has: (0, at[0, k])),
                pl.BlockSpec((width, BW), lambda k, block, at, has: (0, at[1, k])),
                pl.BlockSpec(selected.shape, lambda k, block, at, has: (0, 0)),
                pl.BlockSpec(memory_space=pl.ANY),
            ],
            out_specs=strip,
        ),
        out_shape=jax.ShapeDtypeStruct(base.shape, BF16),
        input_output_aliases={8: 0},
        compiler_params=pltpu.CompilerParams(vmem_limit_bytes=VMEM),
        cost_estimate=pl.CostEstimate(
            flops=2 * rows * width * width,
            bytes_accessed=2 * rows * 4 * width,
            transcendentals=0,
        ),
    )(block, at, has, root, weights, mine, other, selected, base)


FAR, MIDDLE, NEAR = (3, 3, 0, 0), (2, 2, 1, 1), (1, 0, 3, 2)


def up(x, lo, hi):
    return lax.ppermute(x, "col", [(i, i + 1) for i in range(lo, hi + 1)])


def down(x, lo, hi):
    return lax.ppermute(x, "col", [(i, i - 1) for i in range(lo, hi + 1)])


def add(a, b):
    return (a.astype(F32) + b.astype(F32)).astype(BF16)


def line_scatter(chunks, z):
    far, middle, near, own = chunks
    up1, down1 = up(far, 0, 0), down(far, 3, 3)
    up2 = up(add(jnp.where(z == 0, middle, far), up1), 0, 1)
    down2 = down(add(jnp.where(z == 3, middle, far), down1), 2, 3)
    up3 = up(add(jnp.where(z == 1, middle, near), up2), 0, 2)
    down3 = down(add(jnp.where(z == 2, middle, near), down2), 1, 3)
    total = own.astype(F32) + up3.astype(F32) + down3.astype(F32)
    return total.astype(BF16)


def row_scatter(chunk, r, n):
    if n != 4:
        parts = jnp.stack([chunk(i).astype(BF16) for i in range(n)])
        return lax.psum_scatter(parts, "row", scatter_dimension=0, tiled=False).astype(F32)
    arrived = [swap(chunk(r ^ d).astype(BF16), "row", d) for d in (1, 2, 3)]
    return sum((a.astype(F32) for a in arrived), chunk(r).astype(F32))


def row_gather(x, r, n, axis):
    if n != 4:
        return lax.all_gather(x, "row", axis=axis, tiled=True)
    shape = list(x.shape)
    step = shape[axis]
    shape[axis] = step * n
    whole = jnp.zeros(shape, x.dtype)
    for d in range(n):
        piece = swap(x, "row", d) if d else x
        whole = lax.dynamic_update_slice_in_dim(whole, piece, (r ^ d) * step, axis)
    return whole


def col_scatter(x, z):
    n = lax.axis_size("col")
    step = x.shape[0] // n
    piece = lambda i: take(x, i * step, step, 0)
    arrived = [swap(piece(z ^ d).astype(BF16), "col", d) for d in range(1, n)]
    return sum((a.astype(F32) for a in arrived), piece(z)).astype(BF16)


def col_gather(x, z):
    n = lax.axis_size("col")
    step = x.shape[0]
    whole = jnp.zeros((step * n, *x.shape[1:]), x.dtype)
    for d in range(n):
        part = swap(x, "col", d) if d else x
        whole = lax.dynamic_update_slice_in_dim(whole, part, (z ^ d) * step, 0)
    return whole


def symmetric_rows(left, right, axis, strip):
    contract = ((1 - axis,), (1 - axis,))
    if strip % BW:
        return lambda i: mm(take(left, i * strip, strip, axis), right, contract)
    half = left.shape[axis] // BW // 2 + 1
    own = strip // BW
    reach = (own - 1 + half) * BW
    again = lax.slice_in_dim(right, 0, reach - strip, axis=axis)
    longer = jnp.concatenate([right, again], axis=axis)

    def rows(i):
        product = mm(
            take(left, i * strip, strip, axis), take(longer, i * strip, reach, axis), contract
        ).astype(BF16)
        bands = [
            product[b * BW : (b + 1) * BW, b * BW : (b + half) * BW] for b in range(own)
        ]
        return jnp.concatenate(bands, axis=0)

    return rows


def symmetric_whole(rows, strip, r, n):
    whole = row_gather(rows, r, n, 0)
    return whole if strip % BW else unfold(whole)


def program(capacity, root, child_inverse, coupling, child_weights, root_weights, owner, inside):
    g, r, z = lax.axis_index("grp"), lax.axis_index("row"), lax.axis_index("col")
    nrow, ncol = lax.axis_size("row"), lax.axis_size("col")
    root_cols = root.shape[1]
    blocks = root_cols // BW
    factor, links = child_inverse[0], coupling[0]
    weights = child_weights[0].astype(F32)
    share = links.shape[0]
    width = share * ncol
    cols = factor.shape[1]
    sub = cols // nrow
    slots = owner.shape[0]
    count = slots // 2
    order = [jnp.array(t, I32)[z] for t in (FAR, MIDDLE, NEAR)] + [z]

    slot = jnp.arange(slots, dtype=I32)
    same = owner[:, None] == owner[None, :]
    rank = jnp.sum((same & (slot[None, :] < slot[:, None])).astype(I32), axis=1)
    hit = (owner == z)[None, :] & (rank[None, :] == jnp.arange(capacity, dtype=I32)[:, None])
    place = jnp.sum(jnp.where(hit, inside[None, :], 0), axis=1)
    spot = jnp.stack([z ^ d for d in range(ncol)]).astype(I32)
    picked = pick(root, place, spot, ncol)
    pieces = [picked[0]] + [swap(picked[d], "col", d) for d in range(1, ncol)]
    turn = lambda x: jnp.where(g == 0, x, jnp.roll(x, count))
    selected = assemble(pieces, turn(owner) ^ z, turn(rank))

    mine = selected[:, :width]
    both = jnp.concatenate([mine, swap(selected[:, width:], "grp", 1)], axis=0)
    strip = width // nrow
    margin = row_scatter(symmetric_rows(both, both, 1, strip), r, nrow)
    half = share // 2
    rows_all = [lax.all_gather(links[h * half : (h + 1) * half], "col", axis=0) for h in (0, 1)]
    multiply = lambda h: mm(rows_all[h].reshape(width // 2, -1), factor, ((1,), (0,)))
    part_of = lambda x: row_scatter(lambda i: take(x, i * sub, sub, 1), r, nrow).astype(BF16)
    margin, first = lax.optimization_barrier((margin, multiply(0)))
    margin = col_scatter(margin, z)
    first = part_of(first)
    margin, second = lax.optimization_barrier((margin, multiply(1)))
    margin = col_gather(margin, z)
    second = part_of(second)
    solved = jnp.concatenate([first.reshape(ncol, half, sub), second.reshape(ncol, half, sub)], axis=1)
    solved = solved.reshape(width, sub)
    links_all = jnp.concatenate(rows_all, axis=1).reshape(width, -1)
    my_weights = take(weights, r * sub, sub, 0)[None, :]
    scaled = (solved.astype(F32) * my_weights).astype(BF16)
    margin = symmetric_whole(margin, strip, r, nrow)

    def pull(places):
        left = jnp.concatenate([take(margin, q * share, share, 0) for q in places], axis=0)
        part = (2.0 * mm(left, solved, ((1,), (0,))) * my_weights).astype(BF16)
        part = row_gather(part, r, nrow, 1)
        return part, mm(part, factor, ((1,), (1,))).astype(BF16)

    far, to_far = pull(order[:1])
    middle, to_middle = pull(order[1:2])
    rest, to_rest = pull(order[2:])
    grad_links = line_scatter([to_far, to_middle, to_rest[:share], to_rest[share:]], z)
    pulled = jnp.zeros((width, cols), BF16)
    for q, part in zip(order, (far, middle, rest[:share], rest[share:])):
        pulled = lax.dynamic_update_slice_in_dim(pulled, part, q * share, 0)

    grad_factor = mm(links_all, pulled, ((0,), (0,)))
    grad_factor = (grad_factor + 2.0 * factor.astype(F32) * weights[None, :]).astype(BF16)

    adjoint = row_scatter(symmetric_rows(scaled, solved, 0, strip), r, nrow)
    adjoint = symmetric_whole(col_gather(col_scatter(adjoint, z), z), strip, r, nrow)
    adjoint_other = swap(adjoint, "grp", 1)
    band_all = lax.all_gather(after(selected, rows_all[1]), "col", axis=0, tiled=True)
    base = 2.0 * root.astype(F32) * after(root_weights, margin).astype(F32)[None, :]
    here = jnp.where(owner == z, inside, -1).reshape(2, count)
    here = jnp.where(g == 0, here, here[::-1])
    match = here[:, :, None] == jnp.arange(blocks, dtype=I32)[None, None, :]
    has = jnp.any(match, axis=1)
    at = jnp.sum(jnp.where(match, jnp.arange(count, dtype=I32)[None, :, None], 0), axis=1)
    used = jnp.any(has, axis=0)
    total = jnp.sum(used.astype(I32))
    index = jnp.cumsum(used.astype(I32)) - 1
    step = jnp.minimum(jnp.arange(min(capacity, blocks), dtype=I32), jnp.maximum(total - 1, 0))
    chosen = used[None, :] & (index[None, :] == step[:, None])
    of = lambda x: jnp.sum(jnp.where(chosen, x[None, :], 0), axis=1).astype(I32)
    block = of(jnp.arange(blocks, dtype=I32))
    at = jnp.stack([of(at[w]) for w in range(2)])
    has = jnp.stack([of(has[w].astype(I32)) for w in range(2)])
    grad_root = finish(
        base.astype(BF16),
        root,
        root_weights[None, :],
        adjoint,
        adjoint_other,
        band_all,
        block,
        at,
        has,
    )
    return (grad_root, grad_factor[None], grad_links[None])


def local(root, child_inverse, coupling, child_weights, root_weights, parent_blocks):
    blocks = root.shape[1] // BW
    ids = parent_blocks.reshape(-1)
    owner, inside = ids // blocks, ids % blocks
    slots = ids.shape[0]
    usual = slots * 5 // 12
    most = jnp.max(jnp.sum((owner[:, None] == owner[None, :]).astype(I32), axis=1))
    args = (root, child_inverse, coupling, child_weights, root_weights, owner, inside)
    return lax.cond(
        most <= usual,
        functools.partial(program, usual),
        functools.partial(program, slots),
        *args,
    )


def solution(mesh):
    return jax.shard_map(
        local,
        mesh=mesh,
        in_specs=(
            P(("grp", "row"), "col"),
            P("grp", "row", "col"),
            P("grp", "col", "row"),
            P("grp", "col"),
            P("col"),
            P(),
        ),
        out_specs=(P(("grp", "row"), "col"), P("grp", "row", "col"), P("grp", "col", "row")),
        check_vma=False,
    )
```

```python
import functools

import jax
import jax.numpy as jnp
from jax import lax
from jax.experimental import pallas as pl
from jax.experimental.pallas import tpu as pltpu
from jax.sharding import PartitionSpec as P

BW = 128
F32 = jnp.float32
BF16 = jnp.bfloat16
I32 = jnp.int32
VMEM = 48 * 2**20


def mm(a, b, contract):
    return lax.dot_general(a, b, (contract, ((), ())), preferred_element_type=F32)


def take(x, start, size, axis):
    return lax.dynamic_slice_in_dim(x, start, size, axis)


def after(x, *others):
    return lax.optimization_barrier((x, *others))[0]


def swap(x, axis, d):
    n = lax.axis_size(axis)
    return lax.ppermute(x, axis, [(i, i ^ d) for i in range(n)])


def pick_kernel(band, place, spot, root_ref, *outs):
    for d, out in enumerate(outs):
        out[...] = root_ref[pl.ds(pl.multiple_of(spot[d] * band, band), band), :]


def pick(root, place, spot, parts):
    rows, count = root.shape[0], place.shape[0]
    band = rows // parts
    return pl.pallas_call(
        functools.partial(pick_kernel, band),
        grid_spec=pltpu.PrefetchScalarGridSpec(
            num_scalar_prefetch=2,
            grid=(count,),
            in_specs=[pl.BlockSpec((rows, BW), lambda k, place, spot: (0, place[k]))],
            out_specs=[pl.BlockSpec((band, BW), lambda k, place, spot: (0, k))] * parts,
        ),
        out_shape=[jax.ShapeDtypeStruct((band, count * BW), BF16)] * parts,
        cost_estimate=pl.CostEstimate(
            flops=0, bytes_accessed=4 * rows * count * BW, transcendentals=0
        ),
    )(place, spot, root)


def assemble_kernel(source, rank, *refs):
    pieces, out = refs[:-1], refs[-1]
    slots = out.shape[1] // BW
    for s in range(slots):
        for d, piece in enumerate(pieces):

            @pl.when(source[s] == d)
            def _():
                start = pl.multiple_of(rank[s] * BW, BW)
                out[:, s * BW : (s + 1) * BW] = piece[:, pl.ds(start, BW)]


def assemble(pieces, source, rank):
    band, slots = pieces[0].shape[0], source.shape[0]
    whole = lambda shape: pl.BlockSpec(shape, lambda i, source, rank: (0, 0))
    return pl.pallas_call(
        assemble_kernel,
        grid_spec=pltpu.PrefetchScalarGridSpec(
            num_scalar_prefetch=2,
            grid=(1,),
            in_specs=[whole(p.shape) for p in pieces],
            out_specs=whole((band, slots * BW)),
        ),
        out_shape=jax.ShapeDtypeStruct((band, slots * BW), BF16),
        compiler_params=pltpu.CompilerParams(vmem_limit_bytes=VMEM),
        cost_estimate=pl.CostEstimate(
            flops=0, bytes_accessed=6 * band * slots * BW, transcendentals=0
        ),
    )(source, rank, *pieces)


def unfold_kernel(count, half, packed_ref, out_ref):
    i = pl.program_id(0)
    for d in range(half + 1):
        j = lax.rem(i + d, count)
        out_ref[:, pl.ds(pl.multiple_of(j * BW, BW), BW)] = packed_ref[
            pl.ds(pl.multiple_of(i * BW, BW), BW), d * BW : (d + 1) * BW
        ]
    for d in range(1, count - half):
        j = lax.rem(i + count - d, count)
        block = packed_ref[pl.ds(pl.multiple_of(j * BW, BW), BW), d * BW : (d + 1) * BW]
        out_ref[:, pl.ds(pl.multiple_of(j * BW, BW), BW)] = block.T


def unfold(packed):
    width = packed.shape[0]
    count = width // BW
    return pl.pallas_call(
        functools.partial(unfold_kernel, count, count // 2),
        grid=(count,),
        in_specs=[pl.BlockSpec(packed.shape, lambda i: (0, 0))],
        out_specs=pl.BlockSpec((BW, width), lambda i: (i, 0)),
        out_shape=jax.ShapeDtypeStruct((width, width), BF16),
        compiler_params=pltpu.CompilerParams(vmem_limit_bytes=VMEM),
        cost_estimate=pl.CostEstimate(
            flops=0, bytes_accessed=4 * width * width, transcendentals=0
        ),
    )(packed)


def finish_kernel(block, at, has, root_ref, weight_ref, mine_ref, other_ref, all_ref, base, out_ref, total):
    k = pl.program_id(0)
    width = mine_ref.shape[0]

    @pl.when((k == 0) | (block[k] != block[lax.max(k - 1, 0)]))
    def _():
        total[...] = 2.0 * root_ref[...].astype(F32) * weight_ref[...].astype(F32)
        for w, adjoint in enumerate((mine_ref, other_ref)):

            @pl.when(has[w, k] == 1)
            def _():
                lifted = jnp.dot(
                    all_ref[:, w * width : (w + 1) * width],
                    adjoint[...],
                    preferred_element_type=F32,
                )
                total[...] += 2.0 * lifted.astype(BF16).astype(F32)

        out_ref[...] = total[...].astype(BF16)


def finish(base, root, weights, mine, other, selected, block, at, has):
    rows = root.shape[0]
    width = mine.shape[0]
    steps = block.shape[0]
    strip = pl.BlockSpec((rows, BW), lambda k, block, at, has: (0, block[k]))
    return pl.pallas_call(
        finish_kernel,
        grid_spec=pltpu.PrefetchScalarGridSpec(
            num_scalar_prefetch=3,
            grid=(steps,),
            in_specs=[
                strip,
                pl.BlockSpec((1, BW), lambda k, block, at, has: (0, block[k])),
                pl.BlockSpec((width, BW), lambda k, block, at, has: (0, at[0, k])),
                pl.BlockSpec((width, BW), lambda k, block, at, has: (0, at[1, k])),
                pl.BlockSpec(selected.shape, lambda k, block, at, has: (0, 0)),
                pl.BlockSpec(memory_space=pl.ANY),
            ],
            out_specs=strip,
            scratch_shapes=[pltpu.VMEM((rows, BW), F32)],
        ),
        out_shape=jax.ShapeDtypeStruct(base.shape, BF16),
        input_output_aliases={8: 0},
        compiler_params=pltpu.CompilerParams(vmem_limit_bytes=VMEM),
        cost_estimate=pl.CostEstimate(
            flops=2 * rows * width * width,
            bytes_accessed=2 * rows * 4 * width,
            transcendentals=0,
        ),
    )(block, at, has, root, weights, mine, other, selected, base)


FAR, MIDDLE, NEAR = (3, 3, 0, 0), (2, 2, 1, 1), (1, 0, 3, 2)


def up(x, lo, hi):
    return lax.ppermute(x, "col", [(i, i + 1) for i in range(lo, hi + 1)])


def down(x, lo, hi):
    return lax.ppermute(x, "col", [(i, i - 1) for i in range(lo, hi + 1)])


def add(a, b):
    return (a.astype(F32) + b.astype(F32)).astype(BF16)


def row_exchange(chunk, r, n):
    if n != 4:
        parts = jnp.stack([chunk(i).astype(BF16) for i in range(n)])
        return [lax.psum_scatter(parts, "row", scatter_dimension=0, tiled=False)]
    return [chunk(r)] + [swap(chunk(r ^ d).astype(BF16), "row", d) for d in (1, 2, 3)]


def total_of(terms):
    return sum((x.astype(F32) for x in terms[1:]), terms[0].astype(F32))


def row_scatter(chunk, r, n):
    return total_of(row_exchange(chunk, r, n))


def row_gather(x, r, n, axis):
    if n != 4:
        return lax.all_gather(x, "row", axis=axis, tiled=True)
    shape = list(x.shape)
    step = shape[axis]
    shape[axis] = step * n
    whole = jnp.zeros(shape, x.dtype)
    for d in range(n):
        piece = swap(x, "row", d) if d else x
        whole = lax.dynamic_update_slice_in_dim(whole, piece, (r ^ d) * step, axis)
    return whole


def col_scatter(x, z):
    n = lax.axis_size("col")
    step = x.shape[0] // n
    piece = lambda i: take(x, i * step, step, 0)
    arrived = [swap(piece(z ^ d).astype(BF16), "col", d) for d in range(1, n)]
    return sum((a.astype(F32) for a in arrived), piece(z)).astype(BF16)


def col_gather(x, z):
    n = lax.axis_size("col")
    step = x.shape[0]
    whole = jnp.zeros((step * n, *x.shape[1:]), x.dtype)
    for d in range(n):
        part = swap(x, "col", d) if d else x
        whole = lax.dynamic_update_slice_in_dim(whole, part, (z ^ d) * step, 0)
    return whole


def symmetric_rows(left, right, axis, strip):
    contract = ((1 - axis,), (1 - axis,))
    if strip % BW:
        return lambda i: mm(take(left, i * strip, strip, axis), right, contract)
    half = left.shape[axis] // BW // 2 + 1
    own = strip // BW
    reach = (own - 1 + half) * BW
    again = lax.slice_in_dim(right, 0, reach - strip, axis=axis)
    longer = jnp.concatenate([right, again], axis=axis)

    def rows(i):
        product = mm(
            take(left, i * strip, strip, axis), take(longer, i * strip, reach, axis), contract
        ).astype(BF16)
        bands = [
            product[b * BW : (b + 1) * BW, b * BW : (b + half) * BW] for b in range(own)
        ]
        return jnp.concatenate(bands, axis=0)

    return rows


def symmetric_whole(rows, strip, r, n):
    whole = row_gather(rows, r, n, 0)
    return whole if strip % BW else unfold(whole)


def program(capacity, root, child_inverse, coupling, child_weights, root_weights, owner, inside):
    g, r, z = lax.axis_index("grp"), lax.axis_index("row"), lax.axis_index("col")
    nrow, ncol = lax.axis_size("row"), lax.axis_size("col")
    root_cols = root.shape[1]
    blocks = root_cols // BW
    factor, links = child_inverse[0], coupling[0]
    weights = child_weights[0].astype(F32)
    share = links.shape[0]
    width = share * ncol
    cols = factor.shape[1]
    sub = cols // nrow
    slots = owner.shape[0]
    count = slots // 2
    order = [jnp.array(t, I32)[z] for t in (FAR, MIDDLE, NEAR)] + [z]

    slot = jnp.arange(slots, dtype=I32)
    same = owner[:, None] == owner[None, :]
    rank = jnp.sum((same & (slot[None, :] < slot[:, None])).astype(I32), axis=1)
    hit = (owner == z)[None, :] & (rank[None, :] == jnp.arange(capacity, dtype=I32)[:, None])
    place = jnp.sum(jnp.where(hit, inside[None, :], 0), axis=1)
    spot = jnp.stack([z ^ d for d in range(ncol)]).astype(I32)
    picked = pick(root, place, spot, ncol)
    pieces = [picked[0]] + [swap(picked[d], "col", d) for d in range(1, ncol)]
    turn = lambda x: jnp.where(g == 0, x, jnp.roll(x, count))
    base = (2.0 * root.astype(F32) * root_weights.astype(F32)[None, :]).astype(BF16)
    base, *pieces = lax.optimization_barrier((base, *pieces))
    half = share // 2
    rows_all = [lax.all_gather(x, "col", axis=0) for x in (links[:half], links[half:])]
    selected = assemble(pieces, turn(owner) ^ z, turn(rank))

    mine = selected[:, :width]
    both = jnp.concatenate([mine, swap(selected[:, width:], "grp", 1)], axis=0)
    strip = width // nrow
    margin = row_scatter(symmetric_rows(both, both, 1, strip), r, nrow)
    multiply = lambda x: mm(x.reshape(-1, x.shape[-1]), factor, ((1,), (0,)))
    part_of = lambda x: row_scatter(lambda i: take(x, i * sub, sub, 1), r, nrow).astype(BF16)
    band_all = lax.all_gather(after(selected, rows_all[-1]), "col", axis=0, tiled=True)
    margin, first = lax.optimization_barrier((margin, multiply(rows_all[0])))
    margin = col_scatter(margin, z)
    first = part_of(first)
    margin, first, second = lax.optimization_barrier((margin, first, multiply(rows_all[1])))
    margin = col_gather(margin, z)
    second = part_of(second)
    margin = row_gather(margin, r, nrow, 0)
    solved = [first, second]
    margin = margin if strip % BW else unfold(margin)
    solved = jnp.concatenate([x.reshape(ncol, -1, sub) for x in solved], axis=1).reshape(width, sub)
    my_weights = take(weights, r * sub, sub, 0)[None, :]
    scaled = (solved.astype(F32) * my_weights).astype(BF16)

    def pull(places, *before):
        left = jnp.concatenate([take(margin, q * share, share, 0) for q in places], axis=0)
        left = after(left, *before) if before else left
        return (2.0 * mm(left, solved, ((1,), (0,))) * my_weights).astype(BF16)

    def push(part):
        return mm(part, factor, ((1,), (1,))).astype(BF16)

    local_far = pull(order[:1])
    far = row_gather(local_far, r, nrow, 1)
    adjoint = symmetric_rows(after(scaled, local_far), solved, 0, strip)
    adjoint = row_exchange(adjoint, r, nrow)
    local_middle = pull(order[1:2])
    middle = row_gather(local_middle, r, nrow, 1)
    rest = row_gather(pull(order[2:], local_middle), r, nrow, 1)
    to_far = push(far)
    up1, down1 = up(to_far, 0, 0), down(to_far, 3, 3)
    to_middle = push(middle)
    next_up = add(jnp.where(z == 0, to_middle, to_far), up1)
    next_down = add(jnp.where(z == 3, to_middle, to_far), down1)
    next_up, next_down, rest, to_middle, band_all = lax.optimization_barrier(
        (next_up, next_down, rest, to_middle, band_all)
    )
    up2, down2 = up(next_up, 0, 1), down(next_down, 2, 3)
    to_rest = push(rest)
    to_near, own = to_rest[:share], to_rest[share:]
    adjoint = total_of([after(adjoint[0], to_rest), *adjoint[1:]])
    adjoint = col_scatter(adjoint, z)
    last_up = add(jnp.where(z == 1, to_middle, to_near), up2)
    last_down = add(jnp.where(z == 2, to_middle, to_near), down2)
    adjoint, last_up, last_down, own, *rows_all = lax.optimization_barrier(
        (adjoint, last_up, last_down, own, *rows_all)
    )
    up3, down3 = up(last_up, 0, 2), down(last_down, 1, 3)
    adjoint = col_gather(adjoint, z)
    pulled = jnp.zeros((width, cols), BF16)
    for q, part in zip(order, (far, middle, rest[:share], rest[share:])):
        pulled = lax.dynamic_update_slice_in_dim(pulled, part, q * share, 0)
    links_all = jnp.concatenate(rows_all, axis=1).reshape(width, -1)
    grad_factor = mm(links_all, pulled, ((0,), (0,)))
    grad_factor = (grad_factor + 2.0 * factor.astype(F32) * weights[None, :]).astype(BF16)
    adjoint = row_gather(adjoint, r, nrow, 0)
    grad_links = own.astype(F32) + up3.astype(F32) + down3.astype(F32)
    grad_links = grad_links.astype(BF16)
    adjoint, grad_links, grad_factor = lax.optimization_barrier((adjoint, grad_links, grad_factor))
    adjoint = adjoint if strip % BW else unfold(adjoint)
    adjoint_other = swap(adjoint, "grp", 1)
    here = jnp.where(owner == z, inside, -1).reshape(2, count)
    here = jnp.where(g == 0, here, here[::-1])
    match = here[:, :, None] == jnp.arange(blocks, dtype=I32)[None, None, :]
    has = jnp.any(match, axis=1)
    at = jnp.sum(jnp.where(match, jnp.arange(count, dtype=I32)[None, :, None], 0), axis=1)
    used = jnp.any(has, axis=0)
    total = jnp.sum(used.astype(I32))
    index = jnp.cumsum(used.astype(I32)) - 1
    step = jnp.minimum(jnp.arange(min(capacity, blocks), dtype=I32), jnp.maximum(total - 1, 0))
    chosen = used[None, :] & (index[None, :] == step[:, None])
    of = lambda x: jnp.sum(jnp.where(chosen, x[None, :], 0), axis=1).astype(I32)
    block = of(jnp.arange(blocks, dtype=I32))
    at = jnp.stack([of(at[w]) for w in range(2)])
    has = jnp.stack([of(has[w].astype(I32)) for w in range(2)])
    grad_root = finish(
        base,
        root,
        root_weights[None, :],
        adjoint,
        adjoint_other,
        band_all,
        block,
        at,
        has,
    )
    return (grad_root, grad_factor[None], grad_links[None])


def local(root, child_inverse, coupling, child_weights, root_weights, parent_blocks):
    blocks = root.shape[1] // BW
    ids = parent_blocks.reshape(-1)
    owner, inside = ids // blocks, ids % blocks
    slots = ids.shape[0]
    most = jnp.max(jnp.sum((owner[:, None] == owner[None, :]).astype(I32), axis=1))
    args = (root, child_inverse, coupling, child_weights, root_weights, owner, inside)
    sizes = (slots // 3, slots * 5 // 12, slots)
    which = sum((most > size).astype(I32) for size in sizes[:-1])
    return lax.switch(which, [functools.partial(program, size) for size in sizes], *args)


def solution(mesh):
    return jax.shard_map(
        local,
        mesh=mesh,
        in_specs=(
            P(("grp", "row"), "col"),
            P("grp", "row", "col"),
            P("grp", "col", "row"),
            P("grp", "col"),
            P("col"),
            P(),
        ),
        out_specs=(P(("grp", "row"), "col"), P("grp", "row", "col"), P("grp", "col", "row")),
        check_vma=False,
    )
```

```python
import functools

import jax
import jax.numpy as jnp
from jax import lax
from jax.experimental import pallas as pl
from jax.experimental.pallas import tpu as pltpu
from jax.sharding import PartitionSpec as P

BW = 128
F32 = jnp.float32
BF16 = jnp.bfloat16
I32 = jnp.int32
VMEM = 48 * 2**20


def mm(a, b, contract):
    return lax.dot_general(a, b, (contract, ((), ())), preferred_element_type=F32)


def take(x, start, size, axis):
    return lax.dynamic_slice_in_dim(x, start, size, axis)


def after(x, *others):
    return lax.optimization_barrier((x, *others))[0]


def swap(x, axis, d):
    n = lax.axis_size(axis)
    return lax.ppermute(x, axis, [(i, i ^ d) for i in range(n)])


def pick_kernel(band, place, spot, root_ref, *outs):
    for d, out in enumerate(outs):
        out[...] = root_ref[pl.ds(pl.multiple_of(spot[d] * band, band), band), :]


def pick(root, place, spot, parts):
    rows, count = root.shape[0], place.shape[0]
    band = rows // parts
    return pl.pallas_call(
        functools.partial(pick_kernel, band),
        grid_spec=pltpu.PrefetchScalarGridSpec(
            num_scalar_prefetch=2,
            grid=(count,),
            in_specs=[pl.BlockSpec((rows, BW), lambda k, place, spot: (0, place[k]))],
            out_specs=[pl.BlockSpec((band, BW), lambda k, place, spot: (0, k))] * parts,
        ),
        out_shape=[jax.ShapeDtypeStruct((band, count * BW), BF16)] * parts,
        cost_estimate=pl.CostEstimate(
            flops=0, bytes_accessed=4 * rows * count * BW, transcendentals=0
        ),
    )(place, spot, root)


def assemble_kernel(source, rank, *refs):
    pieces, out = refs[:-1], refs[-1]
    slots = out.shape[1] // BW
    for s in range(slots):
        for d, piece in enumerate(pieces):

            @pl.when(source[s] == d)
            def _():
                start = pl.multiple_of(rank[s] * BW, BW)
                out[:, s * BW : (s + 1) * BW] = piece[:, pl.ds(start, BW)]


def assemble(pieces, source, rank):
    band, slots = pieces[0].shape[0], source.shape[0]
    whole = lambda shape: pl.BlockSpec(shape, lambda i, source, rank: (0, 0))
    return pl.pallas_call(
        assemble_kernel,
        grid_spec=pltpu.PrefetchScalarGridSpec(
            num_scalar_prefetch=2,
            grid=(1,),
            in_specs=[whole(p.shape) for p in pieces],
            out_specs=whole((band, slots * BW)),
        ),
        out_shape=jax.ShapeDtypeStruct((band, slots * BW), BF16),
        compiler_params=pltpu.CompilerParams(vmem_limit_bytes=VMEM),
        cost_estimate=pl.CostEstimate(
            flops=0, bytes_accessed=6 * band * slots * BW, transcendentals=0
        ),
    )(source, rank, *pieces)


def unfold_kernel(count, half, packed_ref, out_ref):
    i = pl.program_id(0)
    for d in range(half + 1):
        j = lax.rem(i + d, count)
        out_ref[:, pl.ds(pl.multiple_of(j * BW, BW), BW)] = packed_ref[
            pl.ds(pl.multiple_of(i * BW, BW), BW), d * BW : (d + 1) * BW
        ]
    for d in range(1, count - half):
        j = lax.rem(i + count - d, count)
        block = packed_ref[pl.ds(pl.multiple_of(j * BW, BW), BW), d * BW : (d + 1) * BW]
        out_ref[:, pl.ds(pl.multiple_of(j * BW, BW), BW)] = block.T


def unfold(packed):
    width = packed.shape[0]
    count = width // BW
    return pl.pallas_call(
        functools.partial(unfold_kernel, count, count // 2),
        grid=(count,),
        in_specs=[pl.BlockSpec(packed.shape, lambda i: (0, 0))],
        out_specs=pl.BlockSpec((BW, width), lambda i: (i, 0)),
        out_shape=jax.ShapeDtypeStruct((width, width), BF16),
        compiler_params=pltpu.CompilerParams(vmem_limit_bytes=VMEM),
        cost_estimate=pl.CostEstimate(
            flops=0, bytes_accessed=4 * width * width, transcendentals=0
        ),
    )(packed)


def finish_kernel(block, at, has, root_ref, weight_ref, mine_ref, other_ref, all_ref, base, out_ref, total):
    k = pl.program_id(0)
    width = mine_ref.shape[0]

    @pl.when((k == 0) | (block[k] != block[lax.max(k - 1, 0)]))
    def _():
        total[...] = 2.0 * root_ref[...].astype(F32) * weight_ref[...].astype(F32)
        for w, adjoint in enumerate((mine_ref, other_ref)):

            @pl.when(has[w, k] == 1)
            def _():
                lifted = jnp.dot(
                    all_ref[:, w * width : (w + 1) * width],
                    adjoint[...],
                    preferred_element_type=F32,
                )
                total[...] += 2.0 * lifted.astype(BF16).astype(F32)

        out_ref[...] = total[...].astype(BF16)


def finish(base, root, weights, mine, other, selected, block, at, has):
    rows = root.shape[0]
    width = mine.shape[0]
    steps = block.shape[0]
    strip = pl.BlockSpec((rows, BW), lambda k, block, at, has: (0, block[k]))
    return pl.pallas_call(
        finish_kernel,
        grid_spec=pltpu.PrefetchScalarGridSpec(
            num_scalar_prefetch=3,
            grid=(steps,),
            in_specs=[
                strip,
                pl.BlockSpec((1, BW), lambda k, block, at, has: (0, block[k])),
                pl.BlockSpec((width, BW), lambda k, block, at, has: (0, at[0, k])),
                pl.BlockSpec((width, BW), lambda k, block, at, has: (0, at[1, k])),
                pl.BlockSpec(selected.shape, lambda k, block, at, has: (0, 0)),
                pl.BlockSpec(memory_space=pl.ANY),
            ],
            out_specs=strip,
            scratch_shapes=[pltpu.VMEM((rows, BW), F32)],
        ),
        out_shape=jax.ShapeDtypeStruct(base.shape, BF16),
        input_output_aliases={8: 0},
        compiler_params=pltpu.CompilerParams(vmem_limit_bytes=VMEM),
        cost_estimate=pl.CostEstimate(
            flops=2 * rows * width * width,
            bytes_accessed=2 * rows * 4 * width,
            transcendentals=0,
        ),
    )(block, at, has, root, weights, mine, other, selected, base)


FAR, MIDDLE, NEAR = (3, 3, 0, 0), (2, 2, 1, 1), (1, 0, 3, 2)


def up(x, lo, hi):
    return lax.ppermute(x, "col", [(i, i + 1) for i in range(lo, hi + 1)])


def down(x, lo, hi):
    return lax.ppermute(x, "col", [(i, i - 1) for i in range(lo, hi + 1)])


def add(a, b):
    return (a.astype(F32) + b.astype(F32)).astype(BF16)


def row_exchange(chunk, r, n):
    if n != 4:
        parts = jnp.stack([chunk(i).astype(BF16) for i in range(n)])
        return [lax.psum_scatter(parts, "row", scatter_dimension=0, tiled=False)]
    return [chunk(r)] + [swap(chunk(r ^ d).astype(BF16), "row", d) for d in (1, 2, 3)]


def total_of(terms):
    return sum((x.astype(F32) for x in terms[1:]), terms[0].astype(F32))


def row_scatter(chunk, r, n):
    return total_of(row_exchange(chunk, r, n))


def row_gather(x, r, n, axis):
    if n != 4:
        return lax.all_gather(x, "row", axis=axis, tiled=True)
    shape = list(x.shape)
    step = shape[axis]
    shape[axis] = step * n
    whole = jnp.zeros(shape, x.dtype)
    for d in range(n):
        piece = swap(x, "row", d) if d else x
        whole = lax.dynamic_update_slice_in_dim(whole, piece, (r ^ d) * step, axis)
    return whole


def col_scatter(x, z):
    n = lax.axis_size("col")
    step = x.shape[0] // n
    piece = lambda i: take(x, i * step, step, 0)
    arrived = [swap(piece(z ^ d).astype(BF16), "col", d) for d in range(1, n)]
    return sum((a.astype(F32) for a in arrived), piece(z)).astype(BF16)


def col_gather(x, z):
    n = lax.axis_size("col")
    step = x.shape[0]
    whole = jnp.zeros((step * n, *x.shape[1:]), x.dtype)
    for d in range(n):
        part = swap(x, "col", d) if d else x
        whole = lax.dynamic_update_slice_in_dim(whole, part, (z ^ d) * step, 0)
    return whole


def symmetric_rows(left, right, axis, strip):
    contract = ((1 - axis,), (1 - axis,))
    if strip % BW:
        return lambda i: mm(take(left, i * strip, strip, axis), right, contract)
    half = left.shape[axis] // BW // 2 + 1
    own = strip // BW
    reach = (own - 1 + half) * BW
    again = lax.slice_in_dim(right, 0, reach - strip, axis=axis)
    longer = jnp.concatenate([right, again], axis=axis)

    def rows(i):
        product = mm(
            take(left, i * strip, strip, axis), take(longer, i * strip, reach, axis), contract
        ).astype(BF16)
        bands = [
            product[b * BW : (b + 1) * BW, b * BW : (b + half) * BW] for b in range(own)
        ]
        return jnp.concatenate(bands, axis=0)

    return rows


def symmetric_whole(rows, strip, r, n):
    whole = row_gather(rows, r, n, 0)
    return whole if strip % BW else unfold(whole)


def program(capacity, root, child_inverse, coupling, child_weights, root_weights, owner, inside):
    g, r, z = lax.axis_index("grp"), lax.axis_index("row"), lax.axis_index("col")
    nrow, ncol = lax.axis_size("row"), lax.axis_size("col")
    root_cols = root.shape[1]
    blocks = root_cols // BW
    factor, links = child_inverse[0], coupling[0]
    weights = child_weights[0].astype(F32)
    share = links.shape[0]
    width = share * ncol
    cols = factor.shape[1]
    sub = cols // nrow
    slots = owner.shape[0]
    count = slots // 2
    order = [jnp.array(t, I32)[z] for t in (FAR, MIDDLE, NEAR)] + [z]

    slot = jnp.arange(slots, dtype=I32)
    same = owner[:, None] == owner[None, :]
    rank = jnp.sum((same & (slot[None, :] < slot[:, None])).astype(I32), axis=1)
    hit = (owner == z)[None, :] & (rank[None, :] == jnp.arange(capacity, dtype=I32)[:, None])
    place = jnp.sum(jnp.where(hit, inside[None, :], 0), axis=1)
    spot = jnp.stack([z ^ d for d in range(ncol)]).astype(I32)
    picked = pick(root, place, spot, ncol)
    pieces = [picked[0]] + [swap(picked[d], "col", d) for d in range(1, ncol)]
    turn = lambda x: jnp.where(g == 0, x, jnp.roll(x, count))
    base = (2.0 * root.astype(F32) * root_weights.astype(F32)[None, :]).astype(BF16)
    base, *pieces = lax.optimization_barrier((base, *pieces))
    half = share // 2
    rows_all = [lax.all_gather(x, "col", axis=0) for x in (links[:half], links[half:])]
    selected = assemble(pieces, turn(owner) ^ z, turn(rank))

    mine = selected[:, :width]
    both = jnp.concatenate([mine, swap(selected[:, width:], "grp", 1)], axis=0)
    strip = width // nrow
    margin = row_scatter(symmetric_rows(both, both, 1, strip), r, nrow)
    multiply = lambda x: mm(x.reshape(-1, x.shape[-1]), factor, ((1,), (0,)))
    part_of = lambda x: row_scatter(lambda i: take(x, i * sub, sub, 1), r, nrow).astype(BF16)
    band_all = lax.all_gather(after(selected, rows_all[-1]), "col", axis=0, tiled=True)
    margin, first = lax.optimization_barrier((margin, multiply(rows_all[0])))
    margin = col_scatter(margin, z)
    first = part_of(first)
    margin, first, second = lax.optimization_barrier((margin, first, multiply(rows_all[1])))
    margin = col_gather(margin, z)
    second = part_of(second)
    margin = row_gather(margin, r, nrow, 0)
    solved = [first, second]
    margin = margin if strip % BW else unfold(margin)
    solved = jnp.concatenate([x.reshape(ncol, -1, sub) for x in solved], axis=1).reshape(width, sub)
    my_weights = take(weights, r * sub, sub, 0)[None, :]
    scaled = (solved.astype(F32) * my_weights).astype(BF16)

    def pull(places, *before):
        left = jnp.concatenate([take(margin, q * share, share, 0) for q in places], axis=0)
        left = after(left, *before) if before else left
        return (2.0 * mm(left, solved, ((1,), (0,))) * my_weights).astype(BF16)

    def push(part):
        return mm(part, factor, ((1,), (1,))).astype(BF16)

    local_far = pull(order[:1])
    far = row_gather(local_far, r, nrow, 1)
    adjoint = symmetric_rows(after(scaled, local_far), solved, 0, strip)
    adjoint = row_exchange(adjoint, r, nrow)
    local_middle = pull(order[1:2])
    middle = row_gather(local_middle, r, nrow, 1)
    rest = row_gather(pull(order[2:], local_middle), r, nrow, 1)
    to_far = push(far)
    up1, down1 = up(to_far, 0, 0), down(to_far, 3, 3)
    to_middle = push(middle)
    next_up = add(jnp.where(z == 0, to_middle, to_far), up1)
    next_down = add(jnp.where(z == 3, to_middle, to_far), down1)
    next_up, next_down, rest, to_middle, band_all = lax.optimization_barrier(
        (next_up, next_down, rest, to_middle, band_all)
    )
    up2, down2 = up(next_up, 0, 1), down(next_down, 2, 3)
    to_rest = push(rest)
    to_near, own = to_rest[:share], to_rest[share:]
    adjoint = total_of([after(adjoint[0], to_rest), *adjoint[1:]])
    adjoint = col_scatter(adjoint, z)
    last_up = add(jnp.where(z == 1, to_middle, to_near), up2)
    last_down = add(jnp.where(z == 2, to_middle, to_near), down2)
    adjoint, last_up, last_down, own, *rows_all = lax.optimization_barrier(
        (adjoint, last_up, last_down, own, *rows_all)
    )
    up3, down3 = up(last_up, 0, 2), down(last_down, 1, 3)
    adjoint = col_gather(adjoint, z)
    pulled = jnp.zeros((width, cols), BF16)
    for q, part in zip(order, (far, middle, rest[:share], rest[share:])):
        pulled = lax.dynamic_update_slice_in_dim(pulled, part, q * share, 0)
    links_all = jnp.concatenate(rows_all, axis=1).reshape(width, -1)
    grad_factor = mm(links_all, pulled, ((0,), (0,)))
    grad_factor = (grad_factor + 2.0 * factor.astype(F32) * weights[None, :]).astype(BF16)
    adjoint = row_gather(adjoint, r, nrow, 0)
    grad_links = own.astype(F32) + up3.astype(F32) + down3.astype(F32)
    grad_links = grad_links.astype(BF16)
    adjoint_other = swap(adjoint, "grp", 1)
    adjoint, adjoint_other, grad_links, grad_factor = lax.optimization_barrier(
        (adjoint, adjoint_other, grad_links, grad_factor)
    )
    if strip % BW == 0:
        adjoint, adjoint_other = unfold(adjoint), unfold(adjoint_other)
    here = jnp.where(owner == z, inside, -1).reshape(2, count)
    here = jnp.where(g == 0, here, here[::-1])
    match = here[:, :, None] == jnp.arange(blocks, dtype=I32)[None, None, :]
    has = jnp.any(match, axis=1)
    at = jnp.sum(jnp.where(match, jnp.arange(count, dtype=I32)[None, :, None], 0), axis=1)
    used = jnp.any(has, axis=0)
    total = jnp.sum(used.astype(I32))
    index = jnp.cumsum(used.astype(I32)) - 1
    step = jnp.minimum(jnp.arange(min(capacity, blocks), dtype=I32), jnp.maximum(total - 1, 0))
    chosen = used[None, :] & (index[None, :] == step[:, None])
    of = lambda x: jnp.sum(jnp.where(chosen, x[None, :], 0), axis=1).astype(I32)
    block = of(jnp.arange(blocks, dtype=I32))
    at = jnp.stack([of(at[w]) for w in range(2)])
    has = jnp.stack([of(has[w].astype(I32)) for w in range(2)])
    grad_root = finish(
        base,
        root,
        root_weights[None, :],
        adjoint,
        adjoint_other,
        band_all,
        block,
        at,
        has,
    )
    return (grad_root, grad_factor[None], grad_links[None])


def local(root, child_inverse, coupling, child_weights, root_weights, parent_blocks):
    blocks = root.shape[1] // BW
    ids = parent_blocks.reshape(-1)
    owner, inside = ids // blocks, ids % blocks
    slots = ids.shape[0]
    most = jnp.max(jnp.sum((owner[:, None] == owner[None, :]).astype(I32), axis=1))
    args = (root, child_inverse, coupling, child_weights, root_weights, owner, inside)
    sizes = (slots // 3, slots * 5 // 12, slots)
    which = sum((most > size).astype(I32) for size in sizes[:-1])
    return lax.switch(which, [functools.partial(program, size) for size in sizes], *args)


def solution(mesh):
    return jax.shard_map(
        local,
        mesh=mesh,
        in_specs=(
            P(("grp", "row"), "col"),
            P("grp", "row", "col"),
            P("grp", "col", "row"),
            P("grp", "col"),
            P("col"),
            P(),
        ),
        out_specs=(P(("grp", "row"), "col"), P("grp", "row", "col"), P("grp", "col", "row")),
        check_vma=False,
    )
```
